256 devices in a mesh: dp: 2 (over y_hi), ctx: 16 (over y_lo, x, core), tp: 8 (over z).
Axes of the slice: x: 4, y: 4 (y_hi: 2, y_lo: 2; y = y_hi * 2 + y_lo), z: 8, core: 2. Of those that a mesh axis runs over, the one named last changes fastest.
Arguments:
- streams: bfloat16 [3, 16384, 8192], P(None, ('dp', 'ctx'), 'tp'), parts along dimension 1, may hold values from -6 to 6
- short_taps: float32 [3, 3, 8192], P(None, None, 'tp'), may hold values from -3 to 3
- long_filter: bfloat16 [1024, 512], P(None, 'tp'), may hold values from -2 to 2
Outputs:
- gated: bfloat16 [16384, 8192], P(('dp', 'ctx', 'tp')), parts along dimension 0
The draws below stay inside these ranges and needn't reach their ends.
There are 2 independent parts, one for each index of `dp`. The reference program is written for one: setup_inputs(seed, part) draws one part's arguments, and reference() takes and returns one part's arrays. A program takes and returns all parts, laid end to end along the dimension named above; an argument that names none is the same for every part. Nothing has to cross between parts.
All inputs are finite; a program needn't handle non-finite values.
Results may differ from the reference program's by a relative error of at most 0.0049.
Values may be sent and summed in bfloat16 or wider, within the bound.
A program may use at most 128 MiB of HBM per device.

```python
import jax
import jax.numpy as jnp
from jax import lax

D = 8192
GSIZE = 16
GROUPS = 512
TOKENS = 8192
FLEN = 1024


def draw_long_filter(key, part):
    key = jax.random.fold_in(key, 11)
    rate_key, value_key = jax.random.split(key)
    lag = jnp.arange(FLEN, dtype=jnp.float32)[:, None]
    rate = jnp.exp(jax.random.uniform(rate_key, (1, GROUPS), jnp.float32, jnp.log(0.3), jnp.log(40.0)))
    values = jnp.clip(jax.random.normal(value_key, (FLEN, GROUPS), jnp.float32), -4.0, 4.0)
    scale = jnp.sqrt(2.0 * rate / FLEN)
    return jnp.clip(values * scale * jnp.exp(-rate * lag / FLEN), -2.0, 2.0).astype(jnp.bfloat16)


def levels(stream_key, extent, shards, smallest, top_value):
    loudness, own = 1.0, jax.random.fold_in(stream_key, 6)
    for dim, parts in shards:
        draws = jnp.exp(jax.random.uniform(jax.random.fold_in(own, dim), (parts,), jnp.float32, smallest / len(shards), top_value / len(shards)))
        loudness = loudness * jnp.repeat(draws, extent[dim] // parts).reshape([-1 if axis == dim else 1 for axis in range(len(extent))])
    return loudness


def gaussian(key, dims, deviation, bound, pieces=(), held_as=jnp.bfloat16):
    values = jax.random.normal(key, dims, jnp.float32) * deviation
    if len(pieces) > 0:
        values = levels(key, dims, pieces, -0.22, 0.18) * values
    return jnp.clip(values, min=-bound, max=bound).astype(held_as)


def setup_inputs(seed: int = 0, part: int = 0) -> dict:
    key_of = jax.random.split(jax.random.key(seed), 4)
    own_keys = jax.random.split(jax.random.fold_in(key_of[3], part), 4)
    return {
        "streams": gaussian(own_keys[0], (3, TOKENS, D), 1.0, 6.0, ((1, 16), (2, 8))),
        "short_taps": gaussian(key_of[1], (3, 3, D), 0.6, 3.0, ((2, 8),), jnp.float32),
        "long_filter": draw_long_filter(jax.random.fold_in(key_of[3], 71), part),
    }


def reference(streams, short_taps, long_filter):
    wide = streams.astype(jnp.float32)
    padded = jnp.pad(wide, ((0, 0), (2, 0), (0, 0)))
    features = (short_taps[:, 0][:, None, :] * padded[:, 2:]
                + short_taps[:, 1][:, None, :] * padded[:, 1:-1]
                + short_taps[:, 2][:, None, :] * padded[:, :-2])
    query = features[0]
    mixed_low = (features[1] * features[2]).astype(jnp.bfloat16)
    mixed = lax.optimization_barrier(mixed_low).astype(jnp.float32)
    filt = jnp.repeat(long_filter.astype(jnp.float32), GSIZE, axis=1)
    length = mixed.shape[0]
    width = mixed.shape[1]
    block = min(512, width)
    count = width // block
    signal_blocks = jnp.transpose(mixed.reshape(length, count, block), (1, 0, 2))
    filter_blocks = jnp.transpose(filt.reshape(filt.shape[0], count, block), (1, 0, 2))
    total = 2 * length + filt.shape[0]

    def convolve(pair):
        signal, taps = pair
        spec = jnp.fft.rfft(signal, total, axis=0) * jnp.fft.rfft(taps, total, axis=0)
        return jnp.fft.irfft(spec, total, axis=0)[:length].astype(jnp.float32)

    conv_blocks = lax.map(convolve, (signal_blocks, filter_blocks))
    conv = jnp.transpose(conv_blocks, (1, 0, 2)).reshape(length, width)
    return (query * conv).astype(jnp.bfloat16)
```

```python
import functools

import jax
import jax.numpy as jnp
from jax import lax
from jax.experimental import pallas as pl
from jax.experimental.pallas import tpu as pltpu
from jax.sharding import PartitionSpec as P

LANES = 128
GSIZE = 16
ORDER = (4, 3, 5, 2, 6, 1, 7)
LEAD = 3
MESH = pl.DeviceIdType.MESH


def kernel(
    n_ctx, n_tp, streams, taps_in, filt_in, out,
    sbuf, taps, filt, rows, tails, wide, query, ext, toep, stage,
    load_sem, small_sem, tail_sem, near_send, near_recv, far_send, far_recv,
    relay_send, z_send, z_recv, own_sem,
):
    chunks = sbuf.shape[0]
    length = sbuf.shape[2]
    per_chunk = LANES // GSIZE
    blocks = length // LANES
    taps_len = filt.shape[0]
    spans = taps_len // LANES + 1
    share = out.shape[0]
    i = lax.axis_index("ctx")
    core = lax.rem(i, 2)
    z = lax.axis_index("tp")

    barrier = pltpu.get_barrier_semaphore()
    for hop in (-2, -1, 1, 2):
        @pl.when((i + hop >= 0) & (i + hop < n_ctx))
        def _():
            pl.semaphore_signal(barrier, inc=1, device_id={"ctx": i + hop}, device_id_type=MESH)
    for hop in ORDER:
        pl.semaphore_signal(
            barrier, inc=1, device_id={"tp": lax.rem(z + hop, n_tp)}, device_id_type=MESH
        )

    def load(k):
        lanes = pl.ds(pl.multiple_of(k * LANES, LANES), LANES)
        return pltpu.make_async_copy(streams.at[:, :, lanes], sbuf.at[k], load_sem.at[k])

    filt_load = pltpu.make_async_copy(filt_in, filt, small_sem.at[0])
    taps_load = pltpu.make_async_copy(taps_in, taps, small_sem.at[1])
    filt_load.start()
    taps_load.start()
    for k in range(chunks):
        load(k).start()

    filt_load.wait()
    rows[:, :LANES] = jnp.zeros((rows.shape[0], LANES), jnp.float32)
    for b in range(taps_len // LANES):
        part = filt[LANES * b : LANES * (b + 1), :].astype(jnp.float32)
        rows[:, LANES * (b + 1) : LANES * (b + 2)] = part.T
    rows[:, LANES * spans :] = jnp.zeros((rows.shape[0], LANES), jnp.float32)

    def build(k):
        for g in range(per_chunk):
            row = rows[pl.ds(k * per_chunk + g, 1), :]
            skew = pltpu.roll(
                jnp.broadcast_to(row, (LANES, row.shape[1])), 0, 1, stride=1, stride_axis=0
            ).astype(jnp.bfloat16)
            for o in range(spans):
                toep[k, g, LANES * (spans - 1 - o) : LANES * (spans - o), :] = (
                    skew[:, LANES * (o + 1) : LANES * (o + 2)]
                )

    taps_load.wait()

    total = (
        jnp.minimum(i, 2) + jnp.minimum(n_ctx - 1 - i, 2) + (n_tp - 1)
    )
    pl.semaphore_wait(barrier, total)

    tail = pltpu.make_async_remote_copy(
        src_ref=streams.at[:, length - 16 :, :], dst_ref=tails,
        send_sem=tail_sem.at[0], recv_sem=tail_sem.at[1],
        device_id={"ctx": jnp.minimum(i + 1, n_ctx - 1)}, device_id_type=MESH,
    )

    @pl.when(i + 1 < n_ctx)
    def _():
        tail.start()

    @pl.when(i == 0)
    def _():
        tails[...] = jnp.zeros_like(tails)
        ext[:, 1, :, :] = jnp.zeros((chunks, LANES, length), jnp.bfloat16)

    @pl.when(i < 2)
    def _():
        ext[:, 0, :, :] = jnp.zeros((chunks, LANES, length), jnp.bfloat16)

    build(0)

    @pl.when(i > 0)
    def _():
        tail.wait_recv()

    def near(k):
        return pltpu.make_async_remote_copy(
            src_ref=ext.at[k, 2], dst_ref=ext.at[k, 1],
            send_sem=near_send.at[k], recv_sem=near_recv.at[k],
            device_id={"ctx": jnp.minimum(i + 1, n_ctx - 1)}, device_id_type=MESH,
        )

    def far(k):
        return pltpu.make_async_remote_copy(
            src_ref=ext.at[k, 2], dst_ref=ext.at[k, 0],
            send_sem=far_send.at[k], recv_sem=far_recv.at[k],
            device_id={"ctx": jnp.minimum(i + 2, n_ctx - 1)}, device_id_type=MESH,
        )

    def relay(k):
        return pltpu.make_async_remote_copy(
            src_ref=ext.at[k, 0], dst_ref=ext.at[k, 1],
            send_sem=relay_send.at[k], recv_sem=near_recv.at[k],
            device_id={"ctx": jnp.maximum(i - 1, 0)}, device_id_type=MESH,
        )

    def featurize(k):
        load(k).wait()
        lanes = pl.ds(pl.multiple_of(k * LANES, LANES), LANES)
        for s in range(3):
            wide[s, :8, :] = tails[s, :, lanes].astype(jnp.float32)[8:16]
            wide[s, 8:, :] = sbuf[k, s].astype(jnp.float32)
        tap = [[taps[s, pl.ds(lag, 1), lanes] for lag in range(3)] for s in range(3)]
        for b in range(blocks):
            at = LANES * b + 8
            f = [
                tap[s][0] * wide[s, at : at + LANES, :]
                + tap[s][1] * wide[s, at - 1 : at - 1 + LANES, :]
                + tap[s][2] * wide[s, at - 2 : at - 2 + LANES, :]
                for s in range(3)
            ]
            query[k, LANES * b : LANES * (b + 1), :] = f[0]
            ext[k, 2, :, LANES * b : LANES * (b + 1)] = (f[1] * f[2]).T.astype(jnp.bfloat16)

        @pl.when(i + 2 < n_ctx)
        def _():
            far(k).start()

        @pl.when(core == 0)
        def _():
            near(k).start()

    def z_copy(k, hop):
        peer = lax.rem(z + hop, n_tp)
        lanes = pl.ds(pl.multiple_of((z * chunks + k) * LANES, LANES), LANES)
        return pltpu.make_async_remote_copy(
            src_ref=stage.at[k, pl.ds(pl.multiple_of(peer * share, share), share), :],
            dst_ref=out.at[:, lanes],
            send_sem=z_send.at[k], recv_sem=z_recv.at[k],
            device_id={"tp": peer}, device_id_type=MESH,
        )

    def own_copy(k):
        lanes = pl.ds(pl.multiple_of((z * chunks + k) * LANES, LANES), LANES)
        return pltpu.make_async_copy(
            stage.at[k, pl.ds(pl.multiple_of(z * share, share), share), :],
            out.at[:, lanes], own_sem.at[k],
        )

    def convolve(k):
        @pl.when(i >= 2)
        def _():
            far(k).wait_recv()

        @pl.when((core == 1) & (i >= 2))
        def _():
            relay(k).start()

        @pl.when(i >= 1)
        def _():
            near(k).wait_recv()

        results = []
        for g in range(per_chunk):
            tiles = [
                ext[k, b // blocks, GSIZE * g : GSIZE * (g + 1),
                    LANES * (b % blocks) : LANES * (b % blocks + 1)]
                for b in range(3 * blocks)
            ]
            left = jnp.concatenate(
                [jnp.concatenate(tiles[a : a + spans], axis=1) for a in range(blocks)], axis=0
            )
            results.append(jnp.dot(left, toep[k, g], preferred_element_type=jnp.float32))
        for a in range(blocks):
            conv = jnp.concatenate([r[GSIZE * a : GSIZE * (a + 1)] for r in results], axis=0).T
            at = slice(LANES * a, LANES * (a + 1))
            stage[k, at, :] = (query[k, at, :] * conv).astype(jnp.bfloat16)
        for hop in ORDER:
            z_copy(k, hop).start()
        own_copy(k).start()

    def loop(lower, upper, body):
        lax.fori_loop(lower, upper, lambda k, _: (body(k), 0)[1], 0)

    loop(0, LEAD, featurize)
    loop(1, LEAD, build)

    def both(k):
        convolve(k)
        featurize(k + LEAD)
        build(k + LEAD)

    loop(0, chunks - LEAD, both)
    loop(chunks - LEAD, chunks, convolve)

    @pl.when(i + 1 < n_ctx)
    def _():
        tail.wait_send()

    def drain(k):
        @pl.when(i + 2 < n_ctx)
        def _():
            far(k).wait_send()

        @pl.when(core == 0)
        def _():
            near(k).wait_send()

        @pl.when((core == 1) & (i >= 2))
        def _():
            relay(k).wait_send()

        own_copy(k).wait()
        most = out.at[:, : (n_tp - 1) * LANES]
        pltpu.make_async_copy(most, most, z_send.at[k]).wait()
        pltpu.make_async_copy(most, most, z_recv.at[k]).wait()

    loop(0, chunks, drain)


def solution(mesh):
    n_ctx, n_tp = mesh.shape["ctx"], mesh.shape["tp"]

    def shards(streams, short_taps, long_filter):
        _, length, channels = streams.shape
        taps_len, groups = long_filter.shape
        chunks = channels // LANES
        bf16, f32 = jnp.bfloat16, jnp.float32
        dma = pltpu.SemaphoreType.DMA
        hbm = pl.BlockSpec(memory_space=pl.ANY)
        return pl.pallas_call(
            functools.partial(kernel, n_ctx, n_tp),
            out_shape=jax.ShapeDtypeStruct((length // n_tp, channels * n_tp), bf16),
            in_specs=[hbm] * 3,
            out_specs=hbm,
            scratch_shapes=[
                pltpu.VMEM((chunks, 3, length, LANES), bf16),
                pltpu.VMEM(short_taps.shape, f32),
                pltpu.VMEM(long_filter.shape, bf16),
                pltpu.VMEM((groups, taps_len + 2 * LANES), f32),
                pltpu.VMEM((3, 16, channels), bf16),
                pltpu.VMEM((3, length + 8, LANES), f32),
                pltpu.VMEM((chunks, length, LANES), f32),
                pltpu.VMEM((chunks, 3, LANES, length), bf16),
                pltpu.VMEM((chunks, LANES // GSIZE, taps_len + LANES, LANES), bf16),
                pltpu.VMEM((chunks, length, LANES), bf16),
                dma((chunks,)), dma((2,)), dma((2,)), dma((chunks,)), dma((chunks,)),
                dma((chunks,)), dma((chunks,)), dma((chunks,)), dma((chunks,)),
                dma((chunks,)), dma((chunks,)),
            ],
            compiler_params=pltpu.CompilerParams(
                collective_id=0, has_side_effects=True, vmem_limit_bytes=48 * 2**20
            ),
        )(streams, short_taps, long_filter)

    return jax.shard_map(
        shards,
        mesh=mesh,
        in_specs=(P(None, ("dp", "ctx"), "tp"), P(None, None, "tp"), P(None, "tp")),
        out_specs=P(("dp", "ctx", "tp"), None),
        check_vma=False,
    )
```

```python
import functools

import jax
import jax.numpy as jnp
from jax import lax
from jax.experimental import pallas as pl
from jax.experimental.pallas import tpu as pltpu
from jax.sharding import PartitionSpec as P

LANES = 128
GSIZE = 16
ORDER = (4, 3, 5, 2, 6, 1, 7)
SPLIT = 2
BUILT = 2
MESH = pl.DeviceIdType.MESH


def kernel(
    n_ctx, n_tp, streams, taps_in, filt_in, out,
    sbuf, taps, filt, rows, ends, tail_out, tails, query, ext, toep, stage,
    load_sem, small_sem, tail_sem, near_send, near_recv, far_send, far_recv,
    early_send, early_recv, relay_send, z_send, z_recv, own_sem,
):
    chunks = sbuf.shape[0]
    length = sbuf.shape[2]
    per_chunk = LANES // GSIZE
    blocks = length // LANES
    taps_len = filt.shape[1]
    spans = taps_len // LANES + 1
    share = out.shape[0]
    f32, bf16 = jnp.float32, jnp.bfloat16
    i = lax.axis_index("ctx")
    core = lax.rem(i, 2)
    z = lax.axis_index("tp")

    barrier = pltpu.get_barrier_semaphore()
    for hop in (-1, 1, -2, 2):
        @pl.when((i + hop >= 0) & (i + hop < n_ctx))
        def _():
            pl.semaphore_signal(barrier, inc=1, device_id={"ctx": i + hop}, device_id_type=MESH)
    for hop in ORDER:
        pl.semaphore_signal(
            barrier, inc=1, device_id={"tp": lax.rem(z + hop, n_tp)}, device_id_type=MESH
        )

    def load(k):
        lanes = pl.ds(pl.multiple_of(k * LANES, LANES), LANES)
        return pltpu.make_async_copy(streams.at[:, :, lanes], sbuf.at[k], load_sem.at[k])

    ends_load = pltpu.make_async_copy(streams.at[:, length - 16 :, :], ends, small_sem.at[0])
    taps_load = pltpu.make_async_copy(taps_in, taps, small_sem.at[1])
    filt_load = pltpu.make_async_copy(filt_in, filt, small_sem.at[2])
    ends_load.start()
    load(0).start()
    taps_load.start()
    for k in range(1, chunks):
        load(k).start()
    filt_load.start()

    ends_load.wait()
    row = lax.broadcasted_iota(jnp.int32, (16, ends.shape[2]), 0)
    packed = jnp.zeros(row.shape, f32)
    for s in range(3):
        moved = pltpu.roll(ends[s].astype(f32), 2 * s + 2, 0)
        packed = jnp.where((row == 2 * s) | (row == 2 * s + 1), moved, packed)
    tail_out[...] = packed.astype(bf16)

    @pl.when(i == 0)
    def _():
        tails[...] = jnp.zeros_like(tails)
        ext[:, 1, :, :] = jnp.zeros((chunks, LANES, length), bf16)

    @pl.when(i < 2)
    def _():
        ext[:, 0, :, :] = jnp.zeros((chunks, LANES, length), bf16)

    pl.semaphore_wait(
        barrier, jnp.minimum(i, 2) + jnp.minimum(n_ctx - 1 - i, 2) + (n_tp - 1)
    )

    following = jnp.minimum(i + 1, n_ctx - 1)
    second = jnp.minimum(i + 2, n_ctx - 1)
    tail = pltpu.make_async_remote_copy(
        src_ref=tail_out, dst_ref=tails, send_sem=tail_sem.at[0], recv_sem=tail_sem.at[1],
        device_id={"ctx": following}, device_id_type=MESH,
    )

    @pl.when(i + 1 < n_ctx)
    def _():
        tail.start()

    def near(k):
        return pltpu.make_async_remote_copy(
            src_ref=ext.at[k, 2], dst_ref=ext.at[k, 1],
            send_sem=near_send.at[k], recv_sem=near_recv.at[k],
            device_id={"ctx": following}, device_id_type=MESH,
        )

    def far(k):
        return pltpu.make_async_remote_copy(
            src_ref=ext.at[k, 2], dst_ref=ext.at[k, 0],
            send_sem=far_send.at[k], recv_sem=far_recv.at[k],
            device_id={"ctx": second}, device_id_type=MESH,
        )

    def far_late(k):
        return pltpu.make_async_remote_copy(
            src_ref=ext.at[k, 2, :, :LANES], dst_ref=ext.at[k, 0, :, :LANES],
            send_sem=far_send.at[k], recv_sem=far_recv.at[k],
            device_id={"ctx": second}, device_id_type=MESH,
        )

    def far_early(k):
        return pltpu.make_async_remote_copy(
            src_ref=ext.at[k, 2, :, LANES:], dst_ref=ext.at[k, 0, :, LANES:],
            send_sem=early_send.at[k], recv_sem=early_recv.at[k],
            device_id={"ctx": second}, device_id_type=MESH,
        )

    def relay(k):
        return pltpu.make_async_remote_copy(
            src_ref=ext.at[k, 0], dst_ref=ext.at[k, 1],
            send_sem=relay_send.at[k], recv_sem=near_recv.at[k],
            device_id={"ctx": jnp.maximum(i - 1, 0)}, device_id_type=MESH,
        )

    def featurize(k, which):
        lanes = pl.ds(pl.multiple_of(k * LANES, LANES), LANES)
        tap = [[taps[s, pl.ds(lag, 1), lanes] for lag in range(3)] for s in range(3)]
        for b in which:
            at = slice(LANES * b, LANES * (b + 1))
            f = []
            for s in range(3):
                own = sbuf[k, s, at].astype(f32)
                if b == 0:
                    last = pltpu.roll(tails[:, lanes].astype(f32), 14 - 2 * s, 0)[8:]
                else:
                    last = sbuf[k, s, LANES * b - 16 : LANES * b].astype(f32)[8:]
                both = jnp.concatenate([last, own], axis=0)
                f.append(
                    tap[s][0] * own
                    + tap[s][1] * pltpu.roll(both, 1, 0)[8:]
                    + tap[s][2] * pltpu.roll(both, 2, 0)[8:]
                )
            query[k, at, :] = f[0]
            ext[k, 2, :, at] = (f[1] * f[2]).T.astype(bf16)

    def send_near(k):
        @pl.when(core == 0)
        def _():
            near(k).start()

    def begin(k):
        load(k).wait()
        featurize(k, range(1, blocks))

        @pl.when(i + 2 < n_ctx)
        def _():
            far_early(k).start()

    def finish(k):
        featurize(k, range(1))

        @pl.when(i + 2 < n_ctx)
        def _():
            far_late(k).start()

        send_near(k)

    def whole(k):
        load(k).wait()
        featurize(k, range(blocks))

        @pl.when(i + 2 < n_ctx)
        def _():
            far(k).start()

        send_near(k)

    def build(k):
        for g in range(per_chunk):
            lags = rows[pl.ds(k * per_chunk + g, 1), :]
            skew = pltpu.roll(
                jnp.broadcast_to(lags, (LANES, lags.shape[1])), 0, 1, stride=1, stride_axis=0
            ).astype(bf16)
            for o in range(spans):
                toep[k, g, LANES * (spans - 1 - o) : LANES * (spans - o), :] = (
                    skew[:, LANES * (o + 1) : LANES * (o + 2)]
                )

    def z_copy(k, hop):
        peer = lax.rem(z + hop, n_tp)
        lanes = pl.ds(pl.multiple_of((z * chunks + k) * LANES, LANES), LANES)
        return pltpu.make_async_remote_copy(
            src_ref=stage.at[k, pl.ds(pl.multiple_of(peer * share, share), share), :],
            dst_ref=out.at[:, lanes],
            send_sem=z_send.at[k], recv_sem=z_recv.at[k],
            device_id={"tp": peer}, device_id_type=MESH,
        )

    def own_copy(k):
        lanes = pl.ds(pl.multiple_of((z * chunks + k) * LANES, LANES), LANES)
        return pltpu.make_async_copy(
            stage.at[k, pl.ds(pl.multiple_of(z * share, share), share), :],
            out.at[:, lanes], own_sem.at[k],
        )

    def convolve(k, split):
        @pl.when(i >= 2)
        def _():
            if split:
                far_early(k).wait_recv()
                far_late(k).wait_recv()
            else:
                far(k).wait_recv()

        @pl.when((core == 1) & (i >= 2))
        def _():
            relay(k).start()

        @pl.when(i >= 1)
        def _():
            near(k).wait_recv()

        results = []
        for g in range(per_chunk):
            tiles = [
                ext[k, b // blocks, GSIZE * g : GSIZE * (g + 1),
                    LANES * (b % blocks) : LANES * (b % blocks + 1)]
                for b in range(3 * blocks)
            ]
            left = jnp.concatenate(
                [jnp.concatenate(tiles[a : a + spans], axis=1) for a in range(blocks)], axis=0
            )
            results.append(jnp.dot(left, toep[k, g], preferred_element_type=f32))
        for a in range(blocks):
            conv = jnp.concatenate([r[GSIZE * a : GSIZE * (a + 1)] for r in results], axis=0).T
            at = slice(LANES * a, LANES * (a + 1))
            stage[k, at, :] = (query[k, at, :] * conv).astype(bf16)
        for hop in ORDER:
            z_copy(k, hop).start()
        own_copy(k).start()

    def loop(lower, upper, body):
        lax.fori_loop(lower, upper, lambda k, _: (body(k), 0)[1], 0)

    taps_load.wait()
    loop(0, SPLIT, begin)

    @pl.when(i > 0)
    def _():
        tail.wait_recv()

    loop(0, SPLIT, finish)
    loop(SPLIT, chunks, whole)

    filt_load.wait()
    rows[:, :LANES] = jnp.zeros((rows.shape[0], LANES), f32)
    rows[:, LANES : LANES * spans] = filt[...].astype(f32)
    rows[:, LANES * spans :] = jnp.zeros((rows.shape[0], LANES), f32)
    loop(0, BUILT, build)

    def step(split, k):
        convolve(k, split)

        @pl.when(k + BUILT < chunks)
        def _():
            build(k + BUILT)

    loop(0, SPLIT, functools.partial(step, True))
    loop(SPLIT, chunks, functools.partial(step, False))

    @pl.when(i + 1 < n_ctx)
    def _():
        tail.wait_send()

    def drain_halo(k):
        @pl.when(i + 2 < n_ctx)
        def _():
            far(k).wait_send()

        @pl.when(core == 0)
        def _():
            near(k).wait_send()

        @pl.when((core == 1) & (i >= 2))
        def _():
            relay(k).wait_send()

        own_copy(k).wait()

    def drain_split(k):
        @pl.when(i + 2 < n_ctx)
        def _():
            far_early(k).wait_send()
            far_late(k).wait_send()

        @pl.when(core == 0)
        def _():
            near(k).wait_send()

        @pl.when((core == 1) & (i >= 2))
        def _():
            relay(k).wait_send()

        own_copy(k).wait()

    loop(0, SPLIT, drain_split)
    loop(SPLIT, chunks, drain_halo)

    def drain_z(k):
        most = out.at[:, : (n_tp - 1) * LANES]
        pltpu.make_async_copy(most, most, z_send.at[k]).wait()
        pltpu.make_async_copy(most, most, z_recv.at[k]).wait()

    loop(0, chunks, drain_z)


def solution(mesh):
    n_ctx, n_tp = mesh.shape["ctx"], mesh.shape["tp"]

    def shards(streams, short_taps, long_filter):
        _, length, channels = streams.shape
        taps_len, groups = long_filter.shape
        chunks = channels // LANES
        bf16, f32 = jnp.bfloat16, jnp.float32
        dma = pltpu.SemaphoreType.DMA
        hbm = pl.BlockSpec(memory_space=pltpu.HBM)
        return pl.pallas_call(
            functools.partial(kernel, n_ctx, n_tp),
            out_shape=pltpu.VMEM((length // n_tp, channels * n_tp), bf16),
            in_specs=[hbm] * 3,
            out_specs=pl.BlockSpec(memory_space=pl.ANY),
            scratch_shapes=[
                pltpu.VMEM((chunks, 3, length, LANES), bf16),
                pltpu.VMEM(short_taps.shape, f32),
                pltpu.VMEM((groups, taps_len), bf16),
                pltpu.VMEM((groups, taps_len + 2 * LANES), f32),
                pltpu.VMEM((3, 16, channels), bf16),
                pltpu.VMEM((16, channels), bf16),
                pltpu.VMEM((16, channels), bf16),
                pltpu.VMEM((chunks, length, LANES), f32),
                pltpu.VMEM((chunks, 3, LANES, length), bf16),
                pltpu.VMEM((chunks, LANES // GSIZE, taps_len + LANES, LANES), bf16),
                pltpu.VMEM((chunks, length, LANES), bf16),
                dma((chunks,)), dma((3,)), dma((2,)), dma((chunks,)), dma((chunks,)),
                dma((chunks,)), dma((chunks,)), dma((chunks,)), dma((chunks,)),
                dma((chunks,)), dma((chunks,)), dma((chunks,)), dma((chunks,)),
            ],
            compiler_params=pltpu.CompilerParams(
                collective_id=0, has_side_effects=True, vmem_limit_bytes=56 * 2**20
            ),
        )(streams, short_taps, long_filter.T)

    return jax.shard_map(
        shards,
        mesh=mesh,
        in_specs=(P(None, ("dp", "ctx"), "tp"), P(None, None, "tp"), P(None, "tp")),
        out_specs=P(("dp", "ctx", "tp"), None),
        check_vma=False,
    )
```

```python
import functools

import jax
import jax.numpy as jnp
from jax import lax
from jax.experimental import pallas as pl
from jax.experimental.pallas import tpu as pltpu
from jax.sharding import PartitionSpec as P

LANES = 128
GSIZE = 16
ORDER = (0, 1, 2, 3, 7, 4, 6, 5)
MESH = pl.DeviceIdType.MESH


def kernel(
    n_ctx, n_tp, streams, taps_in, filt_in, out,
    sbuf, taps, filt, rows, ends, tail_out, tails, query, ext, toep, stage,
    load_sem, small_sem, tail_sem, near_send, near_recv, far_send, far_recv,
    early_send, early_recv, relay_send, z_send, z_recv, own_sem,
):
    chunks = sbuf.shape[0]
    length = sbuf.shape[2]
    per_chunk = LANES // GSIZE
    blocks = length // LANES
    taps_len = filt.shape[1]
    spans = taps_len // LANES + 1
    share = out.shape[0]
    f32, bf16 = jnp.float32, jnp.bfloat16
    i = lax.axis_index("ctx")
    core = lax.rem(i, 2)
    z = lax.axis_index("tp")

    barrier = pltpu.get_barrier_semaphore()
    for hop in (-1, 1, -2, 2):
        @pl.when((i + hop >= 0) & (i + hop < n_ctx))
        def _():
            pl.semaphore_signal(barrier, inc=1, device_id={"ctx": i + hop}, device_id_type=MESH)
    for hop in range(1, n_tp):
        pl.semaphore_signal(
            barrier, inc=1, device_id={"tp": lax.rem(z + hop, n_tp)}, device_id_type=MESH
        )

    def load(k):
        lanes = pl.ds(pl.multiple_of(k * LANES, LANES), LANES)
        return pltpu.make_async_copy(streams.at[:, :, lanes], sbuf.at[k], load_sem.at[k])

    ends_load = pltpu.make_async_copy(streams.at[:, length - 16 :, :], ends, small_sem.at[0])
    taps_load = pltpu.make_async_copy(taps_in, taps, small_sem.at[1])
    filt_load = pltpu.make_async_copy(filt_in, filt, small_sem.at[2])
    ends_load.start()
    load(0).start()
    taps_load.start()

    ends_load.wait()
    row = lax.broadcasted_iota(jnp.int32, (16, ends.shape[2]), 0)
    packed = jnp.zeros(row.shape, f32)
    for s in range(3):
        moved = pltpu.roll(ends[s].astype(f32), 2 * s + 2, 0)
        packed = jnp.where((row == 2 * s) | (row == 2 * s + 1), moved, packed)
    tail_out[...] = packed.astype(bf16)

    pl.semaphore_wait(
        barrier, jnp.minimum(i, 2) + jnp.minimum(n_ctx - 1 - i, 2) + (n_tp - 1)
    )

    following = jnp.minimum(i + 1, n_ctx - 1)
    second = jnp.minimum(i + 2, n_ctx - 1)
    tail = pltpu.make_async_remote_copy(
        src_ref=tail_out, dst_ref=tails, send_sem=tail_sem.at[0], recv_sem=tail_sem.at[1],
        device_id={"ctx": following}, device_id_type=MESH,
    )

    @pl.when(i + 1 < n_ctx)
    def _():
        tail.start()

    def near(k):
        return pltpu.make_async_remote_copy(
            src_ref=ext.at[k, 2], dst_ref=ext.at[k, 1],
            send_sem=near_send.at[k], recv_sem=near_recv.at[k],
            device_id={"ctx": following}, device_id_type=MESH,
        )

    def far(k):
        return pltpu.make_async_remote_copy(
            src_ref=ext.at[k, 2], dst_ref=ext.at[k, 0],
            send_sem=far_send.at[k], recv_sem=far_recv.at[k],
            device_id={"ctx": second}, device_id_type=MESH,
        )

    def far_late(k):
        return pltpu.make_async_remote_copy(
            src_ref=ext.at[k, 2, :, :LANES], dst_ref=ext.at[k, 0, :, :LANES],
            send_sem=far_send.at[k], recv_sem=far_recv.at[k],
            device_id={"ctx": second}, device_id_type=MESH,
        )

    def far_early(k):
        return pltpu.make_async_remote_copy(
            src_ref=ext.at[k, 2, :, LANES:], dst_ref=ext.at[k, 0, :, LANES:],
            send_sem=early_send.at[k], recv_sem=early_recv.at[k],
            device_id={"ctx": second}, device_id_type=MESH,
        )

    def relay(k):
        return pltpu.make_async_remote_copy(
            src_ref=ext.at[k, 0], dst_ref=ext.at[k, 1],
            send_sem=relay_send.at[k], recv_sem=near_recv.at[k],
            device_id={"ctx": jnp.maximum(i - 1, 0)}, device_id_type=MESH,
        )

    def featurize(k, which):
        lanes = pl.ds(pl.multiple_of(k * LANES, LANES), LANES)
        tap = [[taps[s, pl.ds(lag, 1), lanes] for lag in range(3)] for s in range(3)]
        for b in which:
            at = slice(LANES * b, LANES * (b + 1))
            f = []
            for s in range(3):
                own = sbuf[k, s, at].astype(f32)
                if b == 0:
                    last = pltpu.roll(tails[:, lanes].astype(f32), 14 - 2 * s, 0)[8:]
                else:
                    last = sbuf[k, s, LANES * b - 16 : LANES * b].astype(f32)[8:]
                both = jnp.concatenate([last, own], axis=0)
                f.append(
                    tap[s][0] * own
                    + tap[s][1] * pltpu.roll(both, 1, 0)[8:]
                    + tap[s][2] * pltpu.roll(both, 2, 0)[8:]
                )
            query[k, at, :] = f[0]
            ext[k, 2, :, at] = (f[1] * f[2]).T.astype(bf16)

    def send_near(k):
        @pl.when(core == 0)
        def _():
            near(k).start()

    def send_far(k):
        @pl.when(i + 2 < n_ctx)
        def _():
            far(k).start()

    ahead = (core == 1) & (i + 2 < n_ctx)
    behind = (core == 0) & (i + 2 < n_ctx)

    def build(k):
        for g in range(per_chunk):
            lags = rows[pl.ds(k * per_chunk + g, 1), :]
            skew = pltpu.roll(
                jnp.broadcast_to(lags, (LANES, lags.shape[1])), 0, 1, stride=1, stride_axis=0
            ).astype(bf16)
            for o in range(spans):
                toep[k, g, LANES * (spans - 1 - o) : LANES * (spans - o), :] = (
                    skew[:, LANES * (o + 1) : LANES * (o + 2)]
                )

    def z_copy(k, hop):
        peer = lax.rem(z + hop, n_tp)
        lanes = pl.ds(pl.multiple_of((z * chunks + k) * LANES, LANES), LANES)
        return pltpu.make_async_remote_copy(
            src_ref=stage.at[k, pl.ds(pl.multiple_of(peer * share, share), share), :],
            dst_ref=out.at[:, lanes],
            send_sem=z_send.at[k], recv_sem=z_recv.at[k],
            device_id={"tp": peer}, device_id_type=MESH,
        )

    def own_copy(k):
        lanes = pl.ds(pl.multiple_of((z * chunks + k) * LANES, LANES), LANES)
        return pltpu.make_async_copy(
            stage.at[k, pl.ds(pl.multiple_of(z * share, share), share), :],
            out.at[:, lanes], own_sem.at[k],
        )

    def arrive(k, first):
        if first:
            @pl.when((core == 1) & (i >= 2))
            def _():
                far_early(k).wait_recv()
                far_late(k).wait_recv()

            @pl.when((core == 0) & (i >= 2))
            def _():
                far(k).wait_recv()
        else:
            @pl.when(i >= 2)
            def _():
                far(k).wait_recv()

        @pl.when((core == 1) & (i >= 2))
        def _():
            relay(k).start()

        @pl.when(i >= 1)
        def _():
            near(k).wait_recv()

    def convolve(k):
        results = []
        for g in range(per_chunk):
            tiles = [
                ext[k, b // blocks, GSIZE * g : GSIZE * (g + 1),
                    LANES * (b % blocks) : LANES * (b % blocks + 1)]
                for b in range(3 * blocks)
            ]
            left = jnp.concatenate(
                [jnp.concatenate(tiles[a : a + spans], axis=1) for a in range(blocks)], axis=0
            )
            results.append(jnp.dot(left, toep[k, g], preferred_element_type=f32))
        for a in range(blocks):
            conv = jnp.concatenate([r[GSIZE * a : GSIZE * (a + 1)] for r in results], axis=0).T
            at = slice(LANES * a, LANES * (a + 1))
            stage[k, at, :] = (query[k, at, :] * conv).astype(bf16)
        own_copy(k).start()

    def loop(lower, upper, body):
        lax.fori_loop(lower, upper, lambda k, _: (body(k), 0)[1], 0)

    taps_load.wait()
    load(0).wait()
    for k in range(1, 3):
        load(k).start()
    filt_load.start()
    featurize(0, range(1, blocks))

    @pl.when(ahead)
    def _():
        far_early(0).start()

    @pl.when(i == 0)
    def _():
        tails[...] = jnp.zeros_like(tails)
        ext[:, 1, :, :] = jnp.zeros((chunks, LANES, length), bf16)

    @pl.when(i < 2)
    def _():
        ext[:, 0, :, :] = jnp.zeros((chunks, LANES, length), bf16)

    load(1).wait()
    for k in range(3, chunks):
        load(k).start()
    featurize(1, range(1, blocks))
    filt_load.wait()
    rows[:, :LANES] = jnp.zeros((rows.shape[0], LANES), f32)
    rows[:, LANES : LANES * spans] = filt[...].astype(f32)
    rows[:, LANES * spans :] = jnp.zeros((rows.shape[0], LANES), f32)

    @pl.when(i > 0)
    def _():
        tail.wait_recv()

    featurize(0, range(1))

    @pl.when(ahead)
    def _():
        far_late(0).start()

    send_near(0)
    featurize(1, range(1))
    send_near(1)
    load(2).wait()
    featurize(2, range(blocks))
    send_near(2)

    @pl.when(behind)
    def _():
        far(0).start()

    build(0)
    send_far(1)
    send_far(2)

    def more(k):
        load(k).wait()
        featurize(k, range(blocks))
        send_far(k)
        send_near(k)

    def send_z(k):
        for peer in ORDER:
            @pl.when(z != peer)
            def _():
                z_copy(k, lax.rem(peer - z + n_tp, n_tp)).start()

    arrive(0, True)
    convolve(0)
    send_z(0)
    more(3)
    build(1)

    def step(k):
        arrive(k, False)
        convolve(k)
        send_z(k)

        @pl.when(k + 3 < chunks)
        def _():
            more(k + 3)

        @pl.when(k + 1 < chunks)
        def _():
            build(k + 1)

    loop(1, chunks, step)

    @pl.when(i + 1 < n_ctx)
    def _():
        tail.wait_send()

    @pl.when(ahead)
    def _():
        far_early(0).wait_send()
        far_late(0).wait_send()

    @pl.when(behind)
    def _():
        far(0).wait_send()

    def drain_far(k):
        @pl.when(i + 2 < n_ctx)
        def _():
            far(k).wait_send()

    def drain_rest(k):
        @pl.when(core == 0)
        def _():
            near(k).wait_send()

        @pl.when((core == 1) & (i >= 2))
        def _():
            relay(k).wait_send()

        own_copy(k).wait()

    loop(1, chunks, drain_far)
    loop(0, chunks, drain_rest)

    def drain_z(k):
        most = out.at[:, : (n_tp - 1) * LANES]
        pltpu.make_async_copy(most, most, z_send.at[k]).wait()
        pltpu.make_async_copy(most, most, z_recv.at[k]).wait()

    loop(0, chunks, drain_z)


def solution(mesh):
    n_ctx, n_tp = mesh.shape["ctx"], mesh.shape["tp"]

    def shards(streams, short_taps, long_filter):
        _, length, channels = streams.shape
        taps_len, groups = long_filter.shape
        chunks = channels // LANES
        bf16, f32 = jnp.bfloat16, jnp.float32
        dma = pltpu.SemaphoreType.DMA
        hbm = pl.BlockSpec(memory_space=pltpu.HBM)
        return pl.pallas_call(
            functools.partial(kernel, n_ctx, n_tp),
            out_shape=pltpu.VMEM((length // n_tp, channels * n_tp), bf16),
            in_specs=[hbm] * 3,
            out_specs=pl.BlockSpec(memory_space=pl.ANY),
            scratch_shapes=[
                pltpu.VMEM((chunks, 3, length, LANES), bf16),
                pltpu.VMEM(short_taps.shape, f32),
                pltpu.VMEM((groups, taps_len), bf16),
                pltpu.VMEM((groups, taps_len + 2 * LANES), f32),
                pltpu.VMEM((3, 16, channels), bf16),
                pltpu.VMEM((16, channels), bf16),
                pltpu.VMEM((16, channels), bf16),
                pltpu.VMEM((chunks, length, LANES), f32),
                pltpu.VMEM((chunks, 3, LANES, length), bf16),
                pltpu.VMEM((chunks, LANES // GSIZE, taps_len + LANES, LANES), bf16),
                pltpu.VMEM((chunks, length, LANES), bf16),
                dma((chunks,)), dma((3,)), dma((2,)), dma((chunks,)), dma((chunks,)),
                dma((chunks,)), dma((chunks,)), dma((chunks,)), dma((chunks,)),
                dma((chunks,)), dma((chunks,)), dma((chunks,)), dma((chunks,)),
            ],
            compiler_params=pltpu.CompilerParams(
                collective_id=0, has_side_effects=True, vmem_limit_bytes=56 * 2**20
            ),
        )(streams, short_taps, long_filter.T)

    return jax.shard_map(
        shards,
        mesh=mesh,
        in_specs=(P(None, ("dp", "ctx"), "tp"), P(None, None, "tp"), P(None, "tp")),
        out_specs=P(("dp", "ctx", "tp"), None),
        check_vma=False,
    )
```

```python
import functools

import jax
import jax.numpy as jnp
from jax import lax
from jax.experimental import pallas as pl
from jax.experimental.pallas import tpu as pltpu
from jax.sharding import PartitionSpec as P

LANES = 128
GSIZE = 16
ORDER = (0, 1, 2, 3, 7, 4, 6, 5)
MESH = pl.DeviceIdType.MESH


def kernel(
    n_ctx, n_tp, streams, taps_in, filt_in, out,
    sbuf, taps, filt, rows, ends, tail_out, tails, query, ext, toep, stage,
    load_sem, small_sem, tail_sem, near_send, near_recv, far_send, far_recv,
    early_send, early_recv, relay_send, z_send, z_recv, own_sem,
):
    chunks = sbuf.shape[0]
    length = sbuf.shape[2]
    per_chunk = LANES // GSIZE
    blocks = length // LANES
    taps_len = filt.shape[1]
    spans = taps_len // LANES + 1
    share = out.shape[0]
    f32, bf16 = jnp.float32, jnp.bfloat16
    i = lax.axis_index("ctx")
    core = lax.rem(i, 2)
    z = lax.axis_index("tp")

    barrier = pltpu.get_barrier_semaphore()
    for hop in (-1, 1, -2, 2):
        @pl.when((i + hop >= 0) & (i + hop < n_ctx))
        def _():
            pl.semaphore_signal(barrier, inc=1, device_id={"ctx": i + hop}, device_id_type=MESH)
    for hop in range(1, n_tp):
        pl.semaphore_signal(
            barrier, inc=1, device_id={"tp": lax.rem(z + hop, n_tp)}, device_id_type=MESH
        )

    def load(k):
        lanes = pl.ds(pl.multiple_of(k * LANES, LANES), LANES)
        return pltpu.make_async_copy(streams.at[:, :, lanes], sbuf.at[k], load_sem.at[k])

    ends_load = pltpu.make_async_copy(streams.at[:, length - 16 :, :], ends, small_sem.at[0])
    taps_load = pltpu.make_async_copy(taps_in, taps, small_sem.at[1])
    filt_load = pltpu.make_async_copy(filt_in, filt, small_sem.at[2])
    ends_load.start()
    load(0).start()
    taps_load.start()

    ends_load.wait()
    row = lax.broadcasted_iota(jnp.int32, (16, ends.shape[2]), 0)
    packed = jnp.zeros(row.shape, f32)
    for s in range(3):
        moved = pltpu.roll(ends[s].astype(f32), 2 * s + 2, 0)
        packed = jnp.where((row == 2 * s) | (row == 2 * s + 1), moved, packed)
    tail_out[...] = packed.astype(bf16)

    pl.semaphore_wait(
        barrier, jnp.minimum(i, 2) + jnp.minimum(n_ctx - 1 - i, 2) + (n_tp - 1)
    )

    following = jnp.minimum(i + 1, n_ctx - 1)
    second = jnp.minimum(i + 2, n_ctx - 1)
    tail = pltpu.make_async_remote_copy(
        src_ref=tail_out, dst_ref=tails, send_sem=tail_sem.at[0], recv_sem=tail_sem.at[1],
        device_id={"ctx": following}, device_id_type=MESH,
    )

    @pl.when(i + 1 < n_ctx)
    def _():
        tail.start()

    def near(k):
        return pltpu.make_async_remote_copy(
            src_ref=ext.at[k, 2], dst_ref=ext.at[k, 1],
            send_sem=near_send.at[k], recv_sem=near_recv.at[k],
            device_id={"ctx": following}, device_id_type=MESH,
        )

    def far(k):
        return pltpu.make_async_remote_copy(
            src_ref=ext.at[k, 2], dst_ref=ext.at[k, 0],
            send_sem=far_send.at[k], recv_sem=far_recv.at[k],
            device_id={"ctx": second}, device_id_type=MESH,
        )

    def far_late(k):
        return pltpu.make_async_remote_copy(
            src_ref=ext.at[k, 2, :, :LANES], dst_ref=ext.at[k, 0, :, :LANES],
            send_sem=far_send.at[k], recv_sem=far_recv.at[k],
            device_id={"ctx": second}, device_id_type=MESH,
        )

    def far_early(k):
        return pltpu.make_async_remote_copy(
            src_ref=ext.at[k, 2, :, LANES:], dst_ref=ext.at[k, 0, :, LANES:],
            send_sem=early_send.at[k], recv_sem=early_recv.at[k],
            device_id={"ctx": second}, device_id_type=MESH,
        )

    def relay(k):
        return pltpu.make_async_remote_copy(
            src_ref=ext.at[k, 0], dst_ref=ext.at[k, 1],
            send_sem=relay_send.at[k], recv_sem=near_recv.at[k],
            device_id={"ctx": jnp.maximum(i - 1, 0)}, device_id_type=MESH,
        )

    def featurize(k, which):
        lanes = pl.ds(pl.multiple_of(k * LANES, LANES), LANES)
        tap = [[taps[s, pl.ds(lag, 1), lanes] for lag in range(3)] for s in range(3)]
        for b in which:
            at = slice(LANES * b, LANES * (b + 1))
            f = []
            for s in range(3):
                own = sbuf[k, s, at].astype(f32)
                if b == 0:
                    last = pltpu.roll(tails[:, lanes].astype(f32), 14 - 2 * s, 0)[8:]
                else:
                    last = sbuf[k, s, LANES * b - 16 : LANES * b].astype(f32)[8:]
                both = jnp.concatenate([last, own], axis=0)
                f.append(
                    tap[s][0] * own
                    + tap[s][1] * pltpu.roll(both, 1, 0)[8:]
                    + tap[s][2] * pltpu.roll(both, 2, 0)[8:]
                )
            query[k, at, :] = f[0]
            ext[k, 2, :, at] = (f[1] * f[2]).T.astype(bf16)

    def send_near(k):
        @pl.when(core == 0)
        def _():
            near(k).start()

    def send_far(k):
        @pl.when(i + 2 < n_ctx)
        def _():
            far(k).start()

    ahead = (core == 1) & (i + 2 < n_ctx)
    behind = (core == 0) & (i + 2 < n_ctx)

    def build(k):
        for g in range(per_chunk):
            lags = rows[pl.ds(k * per_chunk + g, 1), :]
            skew = pltpu.roll(
                jnp.broadcast_to(lags, (LANES, lags.shape[1])), 0, 1, stride=1, stride_axis=0
            ).astype(bf16)
            for o in range(spans):
                toep[k, g, LANES * (spans - 1 - o) : LANES * (spans - o), :] = (
                    skew[:, LANES * (o + 1) : LANES * (o + 2)]
                )

    def z_copy(k, hop):
        peer = lax.rem(z + hop, n_tp)
        lanes = pl.ds(pl.multiple_of((z * chunks + k) * LANES, LANES), LANES)
        return pltpu.make_async_remote_copy(
            src_ref=stage.at[k, pl.ds(pl.multiple_of(peer * share, share), share), :],
            dst_ref=out.at[:, lanes],
            send_sem=z_send.at[k], recv_sem=z_recv.at[k],
            device_id={"tp": peer}, device_id_type=MESH,
        )

    def own_copy(k):
        lanes = pl.ds(pl.multiple_of((z * chunks + k) * LANES, LANES), LANES)
        return pltpu.make_async_copy(
            stage.at[k, pl.ds(pl.multiple_of(z * share, share), share), :],
            out.at[:, lanes], own_sem.at[k],
        )

    def arrive(k, first):
        if first:
            @pl.when((core == 1) & (i >= 2))
            def _():
                far_early(k).wait_recv()
                far_late(k).wait_recv()

            @pl.when((core == 0) & (i >= 2))
            def _():
                far(k).wait_recv()
        else:
            @pl.when(i >= 2)
            def _():
                far(k).wait_recv()

        @pl.when((core == 1) & (i >= 2))
        def _():
            relay(k).start()

        @pl.when(i >= 1)
        def _():
            near(k).wait_recv()

    def convolve(k):
        results = []
        for g in range(per_chunk):
            tiles = [
                ext[k, b // blocks, GSIZE * g : GSIZE * (g + 1),
                    LANES * (b % blocks) : LANES * (b % blocks + 1)]
                for b in range(3 * blocks)
            ]
            left = jnp.concatenate(
                [jnp.concatenate(tiles[a : a + spans], axis=1) for a in range(blocks)], axis=0
            )
            results.append(jnp.dot(left, toep[k, g], preferred_element_type=f32))
        for a in range(blocks):
            conv = jnp.concatenate([r[GSIZE * a : GSIZE * (a + 1)] for r in results], axis=0).T
            at = slice(LANES * a, LANES * (a + 1))
            stage[k, at, :] = (query[k, at, :] * conv).astype(bf16)
        own_copy(k).start()

    def loop(lower, upper, body):
        lax.fori_loop(lower, upper, lambda k, _: (body(k), 0)[1], 0)

    taps_load.wait()
    load(0).wait()
    for k in range(1, 3):
        load(k).start()
    filt_load.start()
    featurize(0, range(1, blocks))

    @pl.when(ahead)
    def _():
        far_early(0).start()

    @pl.when(i == 0)
    def _():
        tails[...] = jnp.zeros_like(tails)
        ext[:, 1, :, :] = jnp.zeros((chunks, LANES, length), bf16)

    @pl.when(i < 2)
    def _():
        ext[:, 0, :, :] = jnp.zeros((chunks, LANES, length), bf16)

    load(1).wait()
    for k in range(3, chunks):
        load(k).start()
    featurize(1, range(1, blocks))
    filt_load.wait()
    rows[:, :LANES] = jnp.zeros((rows.shape[0], LANES), f32)
    rows[:, LANES : LANES * spans] = filt[...].astype(f32)
    rows[:, LANES * spans :] = jnp.zeros((rows.shape[0], LANES), f32)

    @pl.when(i > 0)
    def _():
        tail.wait_recv()

    featurize(0, range(1))

    @pl.when(ahead)
    def _():
        far_late(0).start()

    send_near(0)
    featurize(1, range(1))
    send_near(1)
    load(2).wait()
    featurize(2, range(blocks))
    send_near(2)

    @pl.when(behind)
    def _():
        far(0).start()

    build(0)
    send_far(1)
    send_far(2)

    def more(k):
        load(k).wait()
        featurize(k, range(blocks))
        send_far(k)
        send_near(k)

    def loop_more(lower, upper):
        lax.fori_loop(lower, upper, lambda k, _: (more(k), 0)[1], 0)

    loop_more(3, chunks)

    def send_z(k):
        for peer in ORDER:
            @pl.when(z != peer)
            def _():
                z_copy(k, lax.rem(peer - z + n_tp, n_tp)).start()

    arrive(0, True)
    convolve(0)
    send_z(0)
    build(1)

    def step(k):
        arrive(k, False)
        convolve(k)
        send_z(k)

        @pl.when(k + 1 < chunks)
        def _():
            build(k + 1)

    loop(1, chunks, step)

    @pl.when(i + 1 < n_ctx)
    def _():
        tail.wait_send()

    @pl.when(ahead)
    def _():
        far_early(0).wait_send()
        far_late(0).wait_send()

    @pl.when(behind)
    def _():
        far(0).wait_send()

    def drain_far(k):
        @pl.when(i + 2 < n_ctx)
        def _():
            far(k).wait_send()

    def drain_rest(k):
        @pl.when(core == 0)
        def _():
            near(k).wait_send()

        @pl.when((core == 1) & (i >= 2))
        def _():
            relay(k).wait_send()

        own_copy(k).wait()

    loop(1, chunks, drain_far)
    loop(0, chunks, drain_rest)

    def drain_z(k):
        most = out.at[:, : (n_tp - 1) * LANES]
        pltpu.make_async_copy(most, most, z_send.at[k]).wait()
        pltpu.make_async_copy(most, most, z_recv.at[k]).wait()

    loop(0, chunks, drain_z)


def solution(mesh):
    n_ctx, n_tp = mesh.shape["ctx"], mesh.shape["tp"]

    def shards(streams, short_taps, long_filter):
        _, length, channels = streams.shape
        taps_len, groups = long_filter.shape
        chunks = channels // LANES
        bf16, f32 = jnp.bfloat16, jnp.float32
        dma = pltpu.SemaphoreType.DMA
        hbm = pl.BlockSpec(memory_space=pltpu.HBM)
        return pl.pallas_call(
            functools.partial(kernel, n_ctx, n_tp),
            out_shape=pltpu.VMEM((length // n_tp, channels * n_tp), bf16),
            in_specs=[hbm] * 3,
            out_specs=pl.BlockSpec(memory_space=pl.ANY),
            scratch_shapes=[
                pltpu.VMEM((chunks, 3, length, LANES), bf16),
                pltpu.VMEM(short_taps.shape, f32),
                pltpu.VMEM((groups, taps_len), bf16),
                pltpu.VMEM((groups, taps_len + 2 * LANES), f32),
                pltpu.VMEM((3, 16, channels), bf16),
                pltpu.VMEM((16, channels), bf16),
                pltpu.VMEM((16, channels), bf16),
                pltpu.VMEM((chunks, length, LANES), f32),
                pltpu.VMEM((chunks, 3, LANES, length), bf16),
                pltpu.VMEM((chunks, LANES // GSIZE, taps_len + LANES, LANES), bf16),
                pltpu.VMEM((chunks, length, LANES), bf16),
                dma((chunks,)), dma((3,)), dma((2,)), dma((chunks,)), dma((chunks,)),
                dma((chunks,)), dma((chunks,)), dma((chunks,)), dma((chunks,)),
                dma((chunks,)), dma((chunks,)), dma((chunks,)), dma((chunks,)),
            ],
            compiler_params=pltpu.CompilerParams(
                collective_id=0, has_side_effects=True, vmem_limit_bytes=56 * 2**20
            ),
        )(streams, short_taps, long_filter.T)

    return jax.shard_map(
        shards,
        mesh=mesh,
        in_specs=(P(None, ("dp", "ctx"), "tp"), P(None, None, "tp"), P(None, "tp")),
        out_specs=P(("dp", "ctx", "tp"), None),
        check_vma=False,
    )
```

```python
import functools

import jax
import jax.numpy as jnp
from jax import lax
from jax.experimental import pallas as pl
from jax.experimental.pallas import tpu as pltpu
from jax.sharding import PartitionSpec as P

LANES = 128
GSIZE = 16
ORDER = (0, 1, 2, 3, 7, 4, 6, 5)
MESH = pl.DeviceIdType.MESH


def kernel(
    n_ctx, n_tp, streams, taps_in, filt_in, out,
    sbuf, taps, filt, rows, ends, tail_out, tails, query, ext, toep, stage,
    load_sem, small_sem, tail_sem, near_send, near_recv, far_send, far_recv,
    early_send, early_recv, relay_send, z_send, z_recv, own_sem,
):
    chunks = sbuf.shape[0]
    length = sbuf.shape[2]
    per_chunk = LANES // GSIZE
    blocks = length // LANES
    taps_len = filt.shape[1]
    spans = taps_len // LANES + 1
    share = out.shape[0]
    f32, bf16 = jnp.float32, jnp.bfloat16
    i = lax.axis_index("ctx")
    core = lax.rem(i, 2)
    z = lax.axis_index("tp")

    barrier = pltpu.get_barrier_semaphore()
    for hop in (-1, 1, -2, 2):
        @pl.when((i + hop >= 0) & (i + hop < n_ctx))
        def _():
            pl.semaphore_signal(barrier, inc=1, device_id={"ctx": i + hop}, device_id_type=MESH)
    for hop in range(1, n_tp):
        pl.semaphore_signal(
            barrier, inc=1, device_id={"tp": lax.rem(z + hop, n_tp)}, device_id_type=MESH
        )

    def load(k):
        lanes = pl.ds(pl.multiple_of(k * LANES, LANES), LANES)
        return pltpu.make_async_copy(streams.at[:, :, lanes], sbuf.at[k], load_sem.at[k])

    ends_load = pltpu.make_async_copy(streams.at[:, length - 16 :, :], ends, small_sem.at[0])
    taps_load = pltpu.make_async_copy(taps_in, taps, small_sem.at[1])
    filt_load = pltpu.make_async_copy(filt_in, filt, small_sem.at[2])
    ends_load.start()
    load(0).start()
    taps_load.start()

    ends_load.wait()
    row = lax.broadcasted_iota(jnp.int32, (16, ends.shape[2]), 0)
    packed = jnp.zeros(row.shape, f32)
    for s in range(3):
        moved = pltpu.roll(ends[s].astype(f32), 2 * s + 2, 0)
        packed = jnp.where((row == 2 * s) | (row == 2 * s + 1), moved, packed)
    tail_out[...] = packed.astype(bf16)

    pl.semaphore_wait(
        barrier, jnp.minimum(i, 2) + jnp.minimum(n_ctx - 1 - i, 2) + (n_tp - 1)
    )

    following = jnp.minimum(i + 1, n_ctx - 1)
    second = jnp.minimum(i + 2, n_ctx - 1)
    tail = pltpu.make_async_remote_copy(
        src_ref=tail_out, dst_ref=tails, send_sem=tail_sem.at[0], recv_sem=tail_sem.at[1],
        device_id={"ctx": following}, device_id_type=MESH,
    )

    @pl.when(i + 1 < n_ctx)
    def _():
        tail.start()

    def near(k):
        return pltpu.make_async_remote_copy(
            src_ref=ext.at[k, 2], dst_ref=ext.at[k, 1],
            send_sem=near_send.at[k], recv_sem=near_recv.at[k],
            device_id={"ctx": following}, device_id_type=MESH,
        )

    def far(k):
        return pltpu.make_async_remote_copy(
            src_ref=ext.at[k, 2], dst_ref=ext.at[k, 0],
            send_sem=far_send.at[k], recv_sem=far_recv.at[k],
            device_id={"ctx": second}, device_id_type=MESH,
        )

    def far_late(k):
        return pltpu.make_async_remote_copy(
            src_ref=ext.at[k, 2, :, :LANES], dst_ref=ext.at[k, 0, :, :LANES],
            send_sem=far_send.at[k], recv_sem=far_recv.at[k],
            device_id={"ctx": second}, device_id_type=MESH,
        )

    def far_early(k):
        return pltpu.make_async_remote_copy(
            src_ref=ext.at[k, 2, :, LANES:], dst_ref=ext.at[k, 0, :, LANES:],
            send_sem=early_send.at[k], recv_sem=early_recv.at[k],
            device_id={"ctx": second}, device_id_type=MESH,
        )

    def relay(k):
        return pltpu.make_async_remote_copy(
            src_ref=ext.at[k, 0], dst_ref=ext.at[k, 1],
            send_sem=relay_send.at[k], recv_sem=near_recv.at[k],
            device_id={"ctx": jnp.maximum(i - 1, 0)}, device_id_type=MESH,
        )

    def featurize(k, which):
        lanes = pl.ds(pl.multiple_of(k * LANES, LANES), LANES)
        tap = [[taps[s, pl.ds(lag, 1), lanes] for lag in range(3)] for s in range(3)]
        for b in which:
            at = slice(LANES * b, LANES * (b + 1))
            f = []
            for s in range(3):
                own = sbuf[k, s, at].astype(f32)
                if b == 0:
                    last = pltpu.roll(tails[:, lanes].astype(f32), 14 - 2 * s, 0)[8:]
                else:
                    last = sbuf[k, s, LANES * b - 16 : LANES * b].astype(f32)[8:]
                both = jnp.concatenate([last, own], axis=0)
                f.append(
                    tap[s][0] * own
                    + tap[s][1] * pltpu.roll(both, 1, 0)[8:]
                    + tap[s][2] * pltpu.roll(both, 2, 0)[8:]
                )
            query[k, at, :] = f[0]
            ext[k, 2, :, at] = (f[1] * f[2]).T.astype(bf16)

    def send_near(k):
        @pl.when(core == 0)
        def _():
            near(k).start()

    def send_far(k):
        @pl.when(i + 2 < n_ctx)
        def _():
            far(k).start()

    ahead = i + 2 < n_ctx
    behind = i < -1

    def build(k):
        for g in range(per_chunk):
            lags = rows[pl.ds(k * per_chunk + g, 1), :]
            skew = pltpu.roll(
                jnp.broadcast_to(lags, (LANES, lags.shape[1])), 0, 1, stride=1, stride_axis=0
            ).astype(bf16)
            for o in range(spans):
                toep[k, g, LANES * (spans - 1 - o) : LANES * (spans - o), :] = (
                    skew[:, LANES * (o + 1) : LANES * (o + 2)]
                )

    def z_copy(k, hop):
        peer = lax.rem(z + hop, n_tp)
        lanes = pl.ds(pl.multiple_of((z * chunks + k) * LANES, LANES), LANES)
        return pltpu.make_async_remote_copy(
            src_ref=stage.at[k, pl.ds(pl.multiple_of(peer * share, share), share), :],
            dst_ref=out.at[:, lanes],
            send_sem=z_send.at[k], recv_sem=z_recv.at[k],
            device_id={"tp": peer}, device_id_type=MESH,
        )

    def own_copy(k):
        lanes = pl.ds(pl.multiple_of((z * chunks + k) * LANES, LANES), LANES)
        return pltpu.make_async_copy(
            stage.at[k, pl.ds(pl.multiple_of(z * share, share), share), :],
            out.at[:, lanes], own_sem.at[k],
        )

    def arrive(k, first):
        if first:
            @pl.when(i >= 2)
            def _():
                far_early(k).wait_recv()
                far_late(k).wait_recv()
        else:
            @pl.when(i >= 2)
            def _():
                far(k).wait_recv()

        @pl.when((core == 1) & (i >= 2))
        def _():
            relay(k).start()

        @pl.when(i >= 1)
        def _():
            near(k).wait_recv()

    def convolve(k):
        results = []
        for g in range(per_chunk):
            tiles = [
                ext[k, b // blocks, GSIZE * g : GSIZE * (g + 1),
                    LANES * (b % blocks) : LANES * (b % blocks + 1)]
                for b in range(3 * blocks)
            ]
            left = jnp.concatenate(
                [jnp.concatenate(tiles[a : a + spans], axis=1) for a in range(blocks)], axis=0
            )
            results.append(jnp.dot(left, toep[k, g], preferred_element_type=f32))
        for a in range(blocks):
            conv = jnp.concatenate([r[GSIZE * a : GSIZE * (a + 1)] for r in results], axis=0).T
            at = slice(LANES * a, LANES * (a + 1))
            stage[k, at, :] = (query[k, at, :] * conv).astype(bf16)
        own_copy(k).start()

    def loop(lower, upper, body):
        lax.fori_loop(lower, upper, lambda k, _: (body(k), 0)[1], 0)

    taps_load.wait()
    load(0).wait()
    for k in range(1, 3):
        load(k).start()
    filt_load.start()
    featurize(0, range(1, blocks))

    @pl.when(ahead)
    def _():
        far_early(0).start()

    @pl.when(i == 0)
    def _():
        tails[...] = jnp.zeros_like(tails)
        ext[:, 1, :, :] = jnp.zeros((chunks, LANES, length), bf16)

    @pl.when(i < 2)
    def _():
        ext[:, 0, :, :] = jnp.zeros((chunks, LANES, length), bf16)

    load(1).wait()
    for k in range(3, chunks):
        load(k).start()
    featurize(1, range(1, blocks))
    filt_load.wait()
    rows[:, :LANES] = jnp.zeros((rows.shape[0], LANES), f32)
    rows[:, LANES : LANES * spans] = filt[...].astype(f32)
    rows[:, LANES * spans :] = jnp.zeros((rows.shape[0], LANES), f32)

    @pl.when(i > 0)
    def _():
        tail.wait_recv()

    featurize(0, range(1))

    @pl.when(ahead)
    def _():
        far_late(0).start()

    send_near(0)
    featurize(1, range(1))
    send_near(1)
    load(2).wait()
    featurize(2, range(blocks))
    send_near(2)

    @pl.when(behind)
    def _():
        far(0).start()

    build(0)
    send_far(1)
    send_far(2)

    def more(k):
        load(k).wait()
        featurize(k, range(blocks))
        send_far(k)
        send_near(k)

    def send_z(k):
        for peer in ORDER:
            @pl.when(z != peer)
            def _():
                z_copy(k, lax.rem(peer - z + n_tp, n_tp)).start()

    arrive(0, True)
    convolve(0)
    send_z(0)
    more(3)
    build(1)

    def step(k):
        arrive(k, False)
        convolve(k)
        send_z(k)

        @pl.when(k + 3 < chunks)
        def _():
            more(k + 3)

        @pl.when(k + 1 < chunks)
        def _():
            build(k + 1)

    loop(1, chunks, step)

    @pl.when(i + 1 < n_ctx)
    def _():
        tail.wait_send()

    @pl.when(ahead)
    def _():
        far_early(0).wait_send()
        far_late(0).wait_send()

    @pl.when(behind)
    def _():
        far(0).wait_send()

    def drain_far(k):
        @pl.when(i + 2 < n_ctx)
        def _():
            far(k).wait_send()

    def drain_rest(k):
        @pl.when(core == 0)
        def _():
            near(k).wait_send()

        @pl.when((core == 1) & (i >= 2))
        def _():
            relay(k).wait_send()

        own_copy(k).wait()

    loop(1, chunks, drain_far)
    loop(0, chunks, drain_rest)

    def drain_z(k):
        most = out.at[:, : (n_tp - 1) * LANES]
        pltpu.make_async_copy(most, most, z_send.at[k]).wait()
        pltpu.make_async_copy(most, most, z_recv.at[k]).wait()

    loop(0, chunks, drain_z)


def solution(mesh):
    n_ctx, n_tp = mesh.shape["ctx"], mesh.shape["tp"]

    def shards(streams, short_taps, long_filter):
        _, length, channels = streams.shape
        taps_len, groups = long_filter.shape
        chunks = channels // LANES
        bf16, f32 = jnp.bfloat16, jnp.float32
        dma = pltpu.SemaphoreType.DMA
        hbm = pl.BlockSpec(memory_space=pltpu.HBM)
        return pl.pallas_call(
            functools.partial(kernel, n_ctx, n_tp),
            out_shape=pltpu.VMEM((length // n_tp, channels * n_tp), bf16),
            in_specs=[hbm] * 3,
            out_specs=pl.BlockSpec(memory_space=pl.ANY),
            scratch_shapes=[
                pltpu.VMEM((chunks, 3, length, LANES), bf16),
                pltpu.VMEM(short_taps.shape, f32),
                pltpu.VMEM((groups, taps_len), bf16),
                pltpu.VMEM((groups, taps_len + 2 * LANES), f32),
                pltpu.VMEM((3, 16, channels), bf16),
                pltpu.VMEM((16, channels), bf16),
                pltpu.VMEM((16, channels), bf16),
                pltpu.VMEM((chunks, length, LANES), f32),
                pltpu.VMEM((chunks, 3, LANES, length), bf16),
                pltpu.VMEM((chunks, LANES // GSIZE, taps_len + LANES, LANES), bf16),
                pltpu.VMEM((chunks, length, LANES), bf16),
                dma((chunks,)), dma((3,)), dma((2,)), dma((chunks,)), dma((chunks,)),
                dma((chunks,)), dma((chunks,)), dma((chunks,)), dma((chunks,)),
                dma((chunks,)), dma((chunks,)), dma((chunks,)), dma((chunks,)),
            ],
            compiler_params=pltpu.CompilerParams(
                collective_id=0, has_side_effects=True, vmem_limit_bytes=56 * 2**20
            ),
        )(streams, short_taps, long_filter.T)

    return jax.shard_map(
        shards,
        mesh=mesh,
        in_specs=(P(None, ("dp", "ctx"), "tp"), P(None, None, "tp"), P(None, "tp")),
        out_specs=P(("dp", "ctx", "tp"), None),
        check_vma=False,
    )
```

```python
import functools

import jax
import jax.numpy as jnp
from jax import lax
from jax.experimental import pallas as pl
from jax.experimental.pallas import tpu as pltpu
from jax.sharding import PartitionSpec as P

LANES = 128
GSIZE = 16
ORDER = (0, 1, 2, 3, 7, 4, 6, 5)
MESH = pl.DeviceIdType.MESH


def kernel(
    n_ctx, n_tp, streams, taps_in, filt_in, out,
    sbuf, taps, filt, rows, ends, tail_out, tails, query, ext, toep, stage,
    load_sem, small_sem, tail_sem, near_send, near_recv, far_send, far_recv,
    early_send, early_recv, relay_send, z_send, z_recv, own_sem,
):
    chunks = sbuf.shape[0]
    length = sbuf.shape[2]
    per_chunk = LANES // GSIZE
    blocks = length // LANES
    taps_len = filt.shape[1]
    spans = taps_len // LANES + 1
    share = out.shape[0]
    f32, bf16 = jnp.float32, jnp.bfloat16
    i = lax.axis_index("ctx")
    core = lax.rem(i, 2)
    z = lax.axis_index("tp")

    barrier = pltpu.get_barrier_semaphore()
    for hop in (-1, 1, -2, 2):
        @pl.when((i + hop >= 0) & (i + hop < n_ctx))
        def _():
            pl.semaphore_signal(barrier, inc=1, device_id={"ctx": i + hop}, device_id_type=MESH)
    for hop in range(1, n_tp):
        pl.semaphore_signal(
            barrier, inc=1, device_id={"tp": lax.rem(z + hop, n_tp)}, device_id_type=MESH
        )

    def load(k):
        lanes = pl.ds(pl.multiple_of(k * LANES, LANES), LANES)
        return pltpu.make_async_copy(streams.at[:, :, lanes], sbuf.at[k], load_sem.at[k])

    ends_load = pltpu.make_async_copy(streams.at[:, length - 16 :, :], ends, small_sem.at[0])
    taps_load = pltpu.make_async_copy(taps_in, taps, small_sem.at[1])
    filt_load = pltpu.make_async_copy(filt_in, filt, small_sem.at[2])
    ends_load.start()
    load(0).start()
    taps_load.start()

    ends_load.wait()
    row = lax.broadcasted_iota(jnp.int32, (16, ends.shape[2]), 0)
    packed = jnp.zeros(row.shape, f32)
    for s in range(3):
        moved = pltpu.roll(ends[s].astype(f32), 2 * s + 2, 0)
        packed = jnp.where((row == 2 * s) | (row == 2 * s + 1), moved, packed)
    tail_out[...] = packed.astype(bf16)

    pl.semaphore_wait(
        barrier, jnp.minimum(i, 2) + jnp.minimum(n_ctx - 1 - i, 2) + (n_tp - 1)
    )

    following = jnp.minimum(i + 1, n_ctx - 1)
    second = jnp.minimum(i + 2, n_ctx - 1)
    tail = pltpu.make_async_remote_copy(
        src_ref=tail_out, dst_ref=tails, send_sem=tail_sem.at[0], recv_sem=tail_sem.at[1],
        device_id={"ctx": following}, device_id_type=MESH,
    )

    @pl.when(i + 1 < n_ctx)
    def _():
        tail.start()

    def near(k):
        return pltpu.make_async_remote_copy(
            src_ref=ext.at[k, 2], dst_ref=ext.at[k, 1],
            send_sem=near_send.at[k], recv_sem=near_recv.at[k],
            device_id={"ctx": following}, device_id_type=MESH,
        )

    def far(k):
        return pltpu.make_async_remote_copy(
            src_ref=ext.at[k, 2], dst_ref=ext.at[k, 0],
            send_sem=far_send.at[k], recv_sem=far_recv.at[k],
            device_id={"ctx": second}, device_id_type=MESH,
        )

    def far_late(k):
        return pltpu.make_async_remote_copy(
            src_ref=ext.at[k, 2, :, :LANES], dst_ref=ext.at[k, 0, :, :LANES],
            send_sem=far_send.at[k], recv_sem=far_recv.at[k],
            device_id={"ctx": second}, device_id_type=MESH,
        )

    def far_early(k):
        return pltpu.make_async_remote_copy(
            src_ref=ext.at[k, 2, :, LANES:], dst_ref=ext.at[k, 0, :, LANES:],
            send_sem=early_send.at[k], recv_sem=early_recv.at[k],
            device_id={"ctx": second}, device_id_type=MESH,
        )

    def relay(k):
        return pltpu.make_async_remote_copy(
            src_ref=ext.at[k, 0], dst_ref=ext.at[k, 1],
            send_sem=relay_send.at[k], recv_sem=near_recv.at[k],
            device_id={"ctx": jnp.maximum(i - 1, 0)}, device_id_type=MESH,
        )

    def featurize(k, which):
        lanes = pl.ds(pl.multiple_of(k * LANES, LANES), LANES)
        tap = [[taps[s, pl.ds(lag, 1), lanes] for lag in range(3)] for s in range(3)]
        for b in which:
            at = slice(LANES * b, LANES * (b + 1))
            f = []
            for s in range(3):
                own = sbuf[k, s, at].astype(f32)
                if b == 0:
                    last = pltpu.roll(tails[:, lanes].astype(f32), 14 - 2 * s, 0)[8:]
                else:
                    last = sbuf[k, s, LANES * b - 16 : LANES * b].astype(f32)[8:]
                both = jnp.concatenate([last, own], axis=0)
                f.append(
                    tap[s][0] * own
                    + tap[s][1] * pltpu.roll(both, 1, 0)[8:]
                    + tap[s][2] * pltpu.roll(both, 2, 0)[8:]
                )
            query[k, at, :] = f[0]
            ext[k, 2, :, at] = (f[1] * f[2]).T.astype(bf16)

    def send_near(k):
        @pl.when(core == 0)
        def _():
            near(k).start()

    def crosses(k):
        return (core == 1) & (lax.rem(k, 2) == 1)

    def passes_on(k):
        return (core != lax.rem(k, 2)) & (i >= 2)

    def relay_up(k):
        return pltpu.make_async_remote_copy(
            src_ref=ext.at[k, 1], dst_ref=ext.at[k, 0],
            send_sem=relay_send.at[k], recv_sem=far_recv.at[k],
            device_id={"ctx": following}, device_id_type=MESH,
        )

    def send_far(k):
        @pl.when((i + 2 < n_ctx) & crosses(k))
        def _():
            near(k).start()

        @pl.when((i + 2 < n_ctx) & jnp.logical_not(crosses(k)))
        def _():
            far(k).start()

    ahead = i + 2 < n_ctx
    behind = i < -1

    def build(k):
        for g in range(per_chunk):
            lags = rows[pl.ds(k * per_chunk + g, 1), :]
            skew = pltpu.roll(
                jnp.broadcast_to(lags, (LANES, lags.shape[1])), 0, 1, stride=1, stride_axis=0
            ).astype(bf16)
            for o in range(spans):
                toep[k, g, LANES * (spans - 1 - o) : LANES * (spans - o), :] = (
                    skew[:, LANES * (o + 1) : LANES * (o + 2)]
                )

    def z_copy(k, hop):
        peer = lax.rem(z + hop, n_tp)
        lanes = pl.ds(pl.multiple_of((z * chunks + k) * LANES, LANES), LANES)
        return pltpu.make_async_remote_copy(
            src_ref=stage.at[k, pl.ds(pl.multiple_of(peer * share, share), share), :],
            dst_ref=out.at[:, lanes],
            send_sem=z_send.at[k], recv_sem=z_recv.at[k],
            device_id={"tp": peer}, device_id_type=MESH,
        )

    def own_copy(k):
        lanes = pl.ds(pl.multiple_of((z * chunks + k) * LANES, LANES), LANES)
        return pltpu.make_async_copy(
            stage.at[k, pl.ds(pl.multiple_of(z * share, share), share), :],
            out.at[:, lanes], own_sem.at[k],
        )

    def arrive(k, first):
        if first:
            @pl.when(i >= 2)
            def _():
                far_early(k).wait_recv()
                far_late(k).wait_recv()

            @pl.when((core == 1) & (i >= 2))
            def _():
                relay(k).start()

            @pl.when(i >= 1)
            def _():
                near(k).wait_recv()
        else:
            @pl.when(passes_on(k) & (core == 0))
            def _():
                near(k).wait_recv()
                relay_up(k).start()

            @pl.when(i >= 2)
            def _():
                far(k).wait_recv()

            @pl.when(passes_on(k) & (core == 1))
            def _():
                relay(k).start()

            @pl.when((i >= 1) & jnp.logical_not(passes_on(k) & (core == 0)))
            def _():
                near(k).wait_recv()

    def convolve(k):
        results = []
        for g in range(per_chunk):
            tiles = [
                ext[k, b // blocks, GSIZE * g : GSIZE * (g + 1),
                    LANES * (b % blocks) : LANES * (b % blocks + 1)]
                for b in range(3 * blocks)
            ]
            left = jnp.concatenate(
                [jnp.concatenate(tiles[a : a + spans], axis=1) for a in range(blocks)], axis=0
            )
            results.append(jnp.dot(left, toep[k, g], preferred_element_type=f32))
        for a in range(blocks):
            conv = jnp.concatenate([r[GSIZE * a : GSIZE * (a + 1)] for r in results], axis=0).T
            at = slice(LANES * a, LANES * (a + 1))
            stage[k, at, :] = (query[k, at, :] * conv).astype(bf16)
        own_copy(k).start()

    def loop(lower, upper, body):
        lax.fori_loop(lower, upper, lambda k, _: (body(k), 0)[1], 0)

    taps_load.wait()
    load(0).wait()
    for k in range(1, 3):
        load(k).start()
    filt_load.start()
    featurize(0, range(1, blocks))

    @pl.when(ahead)
    def _():
        far_early(0).start()

    @pl.when(i == 0)
    def _():
        tails[...] = jnp.zeros_like(tails)
        ext[:, 1, :, :] = jnp.zeros((chunks, LANES, length), bf16)

    @pl.when(i < 2)
    def _():
        ext[:, 0, :, :] = jnp.zeros((chunks, LANES, length), bf16)

    load(1).wait()
    for k in range(3, chunks):
        load(k).start()
    featurize(1, range(1, blocks))
    filt_load.wait()
    rows[:, :LANES] = jnp.zeros((rows.shape[0], LANES), f32)
    rows[:, LANES : LANES * spans] = filt[...].astype(f32)
    rows[:, LANES * spans :] = jnp.zeros((rows.shape[0], LANES), f32)

    @pl.when(i > 0)
    def _():
        tail.wait_recv()

    featurize(0, range(1))

    @pl.when(ahead)
    def _():
        far_late(0).start()

    send_near(0)
    featurize(1, range(1))
    send_near(1)
    load(2).wait()
    featurize(2, range(blocks))
    send_near(2)

    @pl.when(behind)
    def _():
        far(0).start()

    build(0)
    send_far(1)
    send_far(2)

    def more(k):
        load(k).wait()
        featurize(k, range(blocks))
        send_far(k)
        send_near(k)

    def send_z(k):
        for peer in ORDER:
            @pl.when(z != peer)
            def _():
                z_copy(k, lax.rem(peer - z + n_tp, n_tp)).start()

    arrive(0, True)
    convolve(0)
    send_z(0)
    more(3)
    build(1)

    def step(k):
        arrive(k, False)
        convolve(k)
        send_z(k)

        @pl.when(k + 3 < chunks)
        def _():
            more(k + 3)

        @pl.when(k + 1 < chunks)
        def _():
            build(k + 1)

    loop(1, chunks, step)

    @pl.when(i + 1 < n_ctx)
    def _():
        tail.wait_send()

    @pl.when(ahead)
    def _():
        far_early(0).wait_send()
        far_late(0).wait_send()

    @pl.when(behind)
    def _():
        far(0).wait_send()

    def drain_far(k):
        @pl.when((i + 2 < n_ctx) & crosses(k))
        def _():
            near(k).wait_send()

        @pl.when((i + 2 < n_ctx) & jnp.logical_not(crosses(k)))
        def _():
            far(k).wait_send()

    def drain_rest(k):
        @pl.when(core == 0)
        def _():
            near(k).wait_send()

        @pl.when(passes_on(k))
        def _():
            relay(k).wait_send()

        own_copy(k).wait()

    loop(1, chunks, drain_far)
    loop(0, chunks, drain_rest)

    def drain_z(k):
        most = out.at[:, : (n_tp - 1) * LANES]
        pltpu.make_async_copy(most, most, z_send.at[k]).wait()
        pltpu.make_async_copy(most, most, z_recv.at[k]).wait()

    loop(0, chunks, drain_z)


def solution(mesh):
    n_ctx, n_tp = mesh.shape["ctx"], mesh.shape["tp"]

    def shards(streams, short_taps, long_filter):
        _, length, channels = streams.shape
        taps_len, groups = long_filter.shape
        chunks = channels // LANES
        bf16, f32 = jnp.bfloat16, jnp.float32
        dma = pltpu.SemaphoreType.DMA
        hbm = pl.BlockSpec(memory_space=pltpu.HBM)
        return pl.pallas_call(
            functools.partial(kernel, n_ctx, n_tp),
            out_shape=pltpu.VMEM((length // n_tp, channels * n_tp), bf16),
            in_specs=[hbm] * 3,
            out_specs=pl.BlockSpec(memory_space=pl.ANY),
            scratch_shapes=[
                pltpu.VMEM((chunks, 3, length, LANES), bf16),
                pltpu.VMEM(short_taps.shape, f32),
                pltpu.VMEM((groups, taps_len), bf16),
                pltpu.VMEM((groups, taps_len + 2 * LANES), f32),
                pltpu.VMEM((3, 16, channels), bf16),
                pltpu.VMEM((16, channels), bf16),
                pltpu.VMEM((16, channels), bf16),
                pltpu.VMEM((chunks, length, LANES), f32),
                pltpu.VMEM((chunks, 3, LANES, length), bf16),
                pltpu.VMEM((chunks, LANES // GSIZE, taps_len + LANES, LANES), bf16),
                pltpu.VMEM((chunks, length, LANES), bf16),
                dma((chunks,)), dma((3,)), dma((2,)), dma((chunks,)), dma((chunks,)),
                dma((chunks,)), dma((chunks,)), dma((chunks,)), dma((chunks,)),
                dma((chunks,)), dma((chunks,)), dma((chunks,)), dma((chunks,)),
            ],
            compiler_params=pltpu.CompilerParams(
                collective_id=0, has_side_effects=True, vmem_limit_bytes=56 * 2**20
            ),
        )(streams, short_taps, long_filter.T)

    return jax.shard_map(
        shards,
        mesh=mesh,
        in_specs=(P(None, ("dp", "ctx"), "tp"), P(None, None, "tp"), P(None, "tp")),
        out_specs=P(("dp", "ctx", "tp"), None),
        check_vma=False,
    )
```
